1024 devices in a mesh: dp: 256 (over x, z_hi, y, core), group: 4 (over z_lo).
Axes of the slice: x: 4, y: 8, z: 16 (z_hi: 4, z_lo: 4; z = z_hi * 4 + z_lo), core: 2. Of those that a mesh axis runs over, the one named last changes fastest.
Arguments:
- image_emb: bfloat16 [262144, 1152], P(('dp', 'group')), may hold values from -0.1796875 to 0.1796875
- text_emb: bfloat16 [262144, 1152], P(('dp', 'group')), may hold values from -0.1796875 to 0.1796875
- scale: float32 [1], replicated, may hold values from 4 to 12
- bias: float32 [1], replicated, may hold values from -4 to -1
Outputs:
- row_loss: float32 [262144], P(('dp', 'group'))
- grad_image: float32 [262144, 1152], P(('dp', 'group'))
- grad_text: float32 [262144, 1152], P(('dp', 'group'))
The draws below stay inside these ranges and needn't reach their ends.
All inputs are finite; a program needn't handle non-finite values.
Results may differ from the reference program's by a relative error of at most 0.0039.
Values may be sent and summed in bfloat16 or wider, within the bound.
No kernel may reach another device: no remote copies, remote signals or barrier semaphores. Data moves between devices by JAX's collectives and lax.ppermute only.
A program may use at most 32 MiB of HBM per device.

```python
import math
import jax
import jax.numpy as jnp
from jax import lax

D = 1152
ROWS = 256
HOPS = 4
PAIRS = 262144
N_DP = 256
N_GROUP = 4


def block_levels(own_key, dims, shards, least, largest):
    gain, own = 1.0, jax.random.fold_in(own_key, 6)
    for dim, blocks in shards:
        heights = jnp.exp(jax.random.uniform(jax.random.fold_in(own, dim), (blocks,), jnp.float32, least / len(shards), largest / len(shards)))
        gain = gain * jnp.repeat(heights, dims[dim] // blocks).reshape([-1 if axis == dim else 1 for axis in range(len(dims))])
    return gain


def gaussian(key, dims, deviation, most, split=(), kind=jnp.bfloat16):
    entries = jax.random.normal(key, dims, jnp.float32) * deviation
    if len(split) > 0:
        entries = block_levels(key, dims, split, -0.22, 0.18) * entries
    return jnp.clip(entries, min=-most, max=most).astype(kind)


def setup_inputs(seed: int = 0) -> dict:
    arg_keys = jax.random.split(jax.random.key(seed), 5)
    return {
        "image_emb": gaussian(arg_keys[0], (PAIRS, D), 0.03, 0.1796875, ((0, 1024),)),
        "text_emb": gaussian(arg_keys[1], (PAIRS, D), 0.03, 0.1796875, ((0, 1024),)),
        "scale": jnp.clip(jnp.exp(jax.random.uniform(arg_keys[2], (1,), jnp.float32, math.log(4.0), math.log(12.0))), 4.0, 12.0),
        "bias": jnp.clip(jax.random.uniform(arg_keys[3], (1,), jnp.float32, -4.0, -1.0), -4.0, -1.0),
    }


def unit_rows(emb):
    values = emb.astype(jnp.float32)
    norm = jnp.sqrt(lax.optimization_barrier(jnp.sum(values * values, axis=-1, keepdims=True)) + 1e-06)
    return (values / norm, norm)

def back_norm(grad, unit, norm):
    return (grad - unit * lax.optimization_barrier(jnp.sum(unit * grad, axis=-1, keepdims=True))) / norm

def rounded(values):
    low = lax.optimization_barrier(values.astype(jnp.bfloat16))
    return low.astype(jnp.float32)

def reference(image_emb, text_emb, scale, bias):
    count = N_DP * N_GROUP
    image_unit, image_norm = unit_rows(image_emb)
    text_unit, text_norm = unit_rows(text_emb)
    image_bf = rounded(image_unit).reshape(count, ROWS, D)
    text_bf = rounded(text_unit).reshape(count, ROWS, D)
    s_val = scale[0]
    b_val = bias[0]
    diagonal = jnp.eye(ROWS, dtype=jnp.float32)
    grad_x = jnp.zeros((count, ROWS, D), jnp.float32)
    grad_y = jnp.zeros((count, ROWS, D), jnp.float32)
    losses = jnp.zeros((count, ROWS), jnp.float32)
    for step in range(HOPS):
        texts = jnp.roll(text_bf, step, axis=0)
        logits = s_val * jnp.einsum('krd,kqd->krq', image_bf, texts) + b_val
        if step == 0:
            sign = 2.0 * diagonal - 1.0
        else:
            sign = -jnp.ones((ROWS, ROWS), jnp.float32)
        losses = losses + lax.optimization_barrier(jnp.sum(jax.nn.softplus(-sign * logits), axis=-1))
        coef = rounded(-sign * jax.nn.sigmoid(-sign * logits))
        grad_x = grad_x + s_val * jnp.einsum('krq,kqd->krd', coef, texts)
        back = s_val * jnp.einsum('krq,krd->kqd', coef, image_bf)
        grad_y = grad_y + jnp.roll(back, -step, axis=0)
    row_loss = losses.reshape(count * ROWS) / (HOPS * ROWS)
    grad_image = back_norm(grad_x.reshape(count * ROWS, D), image_unit, image_norm)
    grad_text = back_norm(grad_y.reshape(count * ROWS, D), text_unit, text_norm)
    return (row_loss, grad_image, grad_text)
```

```python
import jax
import jax.numpy as jnp
from jax import lax
from jax.sharding import PartitionSpec as P

HOPS = 4
GROUP = 4
AXES = ("dp", "group")


def routes(lines):
    def at(line, place):
        return (line % lines) * GROUP + place

    text, near, far = [], [], []
    for line in range(lines):
        text += [
            (at(line, 0), at(line, 1)),
            (at(line, 1), at(line + 1, 0)),
            (at(line, 3), at(line, 2)),
            (at(line, 2), at(line, 3)),
        ]
        near += [
            (at(line, 2), at(line, 1)),
            (at(line + 1, 1), at(line, 2)),
        ]
        far += [
            (at(line, 3), at(line, 1)),
            (at(line + 1, 0), at(line, 2)),
            (at(line, 1), at(line, 0)),
            (at(line + 1, 2), at(line, 3)),
        ]
    return (text, near, far)


def back(pairs):
    return [(target, source) for source, target in pairs]


def unit_rows(emb):
    values = emb.astype(jnp.float32)
    norm = jnp.sqrt(jnp.sum(values * values, axis=-1, keepdims=True) + 1e-06)
    return (values / norm, norm)


def unit_bf(emb):
    return unit_rows(emb)[0].astype(jnp.bfloat16)


def back_norm(grad, unit, norm):
    return (grad - unit * jnp.sum(unit * grad, axis=-1, keepdims=True)) / norm


def rows_by_rows(a, b):
    return lax.dot_general(a, b, (((1,), (1,)), ((), ())), preferred_element_type=jnp.float32)


def columns_by_rows(a, b):
    return lax.dot_general(a, b, (((0,), (0,)), ((), ())), preferred_element_type=jnp.float32)


def off_terms(images, texts, s_val, b_val, keep):
    logits = s_val * rows_by_rows(images, texts) + b_val
    loss = jnp.sum(jax.nn.softplus(logits), axis=-1)
    coef = jax.nn.sigmoid(logits).astype(jnp.bfloat16)
    return (jnp.where(keep, coef, 0), jnp.where(keep, loss, 0.0))


def own_terms(images, texts, s_val, b_val):
    logits = s_val * rows_by_rows(images, texts) + b_val
    rows = images.shape[0]
    upper = lax.broadcasted_iota(jnp.int32, (rows, rows), 0)
    lower = lax.broadcasted_iota(jnp.int32, (rows, rows), 1)
    sign = jnp.where(upper == lower, 1.0, -1.0).astype(jnp.float32)
    loss = jnp.sum(jax.nn.softplus(-sign * logits), axis=-1)
    coef = (-sign * jax.nn.sigmoid(-sign * logits)).astype(jnp.bfloat16)
    return (coef, loss)


def shards(image_emb, text_emb, scale, bias):
    text_way, near_way, far_way = routes(lax.axis_size("dp"))
    place = lax.axis_index("group")
    hub = (place == 1) | (place == 2)
    s_val = scale[0]
    b_val = bias[0]
    rows = image_emb.shape[0]

    near_raw = lax.ppermute(image_emb, AXES, near_way)
    text_raw = lax.ppermute(text_emb, AXES, text_way)
    far_raw = lax.ppermute(image_emb, AXES, far_way)

    image_unit, image_norm = unit_rows(image_emb)
    text_unit, text_norm = unit_rows(text_emb)
    images = image_unit.astype(jnp.bfloat16)
    texts = text_unit.astype(jnp.bfloat16)
    coef, loss = own_terms(images, texts, s_val, b_val)
    grad_x = jnp.dot(coef, texts, preferred_element_type=jnp.float32)
    grad_y = columns_by_rows(coef, images)

    other = unit_bf(text_raw)
    near = jnp.where(hub, unit_bf(near_raw), images)
    far = unit_bf(far_raw)

    c_on, l_on = off_terms(near, texts, s_val, b_val, hub)
    c_rn, l_rn = off_terms(near, other, s_val, b_val, True)
    grad_near = s_val * (
        jnp.dot(c_on, texts, preferred_element_type=jnp.float32)
        + jnp.dot(c_rn, other, preferred_element_type=jnp.float32)
    )
    loss_near = l_on + l_rn
    near_back = lax.ppermute(grad_near.astype(jnp.bfloat16), AXES, back(near_way))

    c_of, l_of = off_terms(far, texts, s_val, b_val, True)
    c_rf, l_rf = off_terms(far, other, s_val, b_val, hub)
    grad_far = s_val * (
        jnp.dot(c_of, texts, preferred_element_type=jnp.float32)
        + jnp.dot(c_rf, other, preferred_element_type=jnp.float32)
    )
    far_back = lax.ppermute(grad_far.astype(jnp.bfloat16), AXES, back(far_way))
    grad_other = s_val * (columns_by_rows(c_rn, near) + columns_by_rows(c_rf, far))
    text_back = lax.ppermute(grad_other.astype(jnp.bfloat16), AXES, back(text_way))
    loss_near_back = lax.ppermute(loss_near, AXES, back(near_way))
    loss_far_back = lax.ppermute(l_of + l_rf, AXES, back(far_way))

    grad_y = s_val * (grad_y + columns_by_rows(c_on, near) + columns_by_rows(c_of, far))
    grad_y = grad_y + text_back.astype(jnp.float32)
    grad_x = s_val * grad_x + jnp.where(hub, near_back.astype(jnp.float32), grad_near)
    grad_x = grad_x + far_back.astype(jnp.float32)
    loss = loss + jnp.where(hub, loss_near_back, loss_near) + loss_far_back
    row_loss = loss / (HOPS * rows)
    grad_image = back_norm(grad_x, image_unit, image_norm)
    grad_text = back_norm(grad_y, text_unit, text_norm)
    return (row_loss, grad_image, grad_text)


def solution(mesh):
    in_specs = (P(("dp", "group"), None), P(("dp", "group"), None), P(), P())
    out_specs = (P(("dp", "group")), P(("dp", "group"), None), P(("dp", "group"), None))
    return jax.shard_map(shards, mesh=mesh, in_specs=in_specs, out_specs=out_specs, check_vma=False)
```

```python
import jax
import jax.numpy as jnp
from jax import lax
from jax.sharding import PartitionSpec as P

HOPS = 4
GROUP = 4
RUN = 16
AXES = ("dp", "group")


def routes(lines):
    def at(line, place):
        return (line % lines) * GROUP + place

    text, near, far = [], [], []
    for line in range(lines):
        text += [(at(line, 0), at(line, 1)), (at(line, 2), at(line, 3))]
        near += [(at(line, 2), at(line, 1))]
        far += [(at(line, 3), at(line, 1))]
        far += [(at(line + 1, 0), at(line, 2))]
        if line % RUN == RUN - 1:
            text += [(at(line, 3), at(line + 1, 0)), (at(line, 1), at(line, 2))]
            near += [(at(line + 1, 0), at(line, 3)), (at(line + 1, 1), at(line + 1, 0))]
            far += [(at(line + 1, 1), at(line, 3)), (at(line + 1, 2), at(line + 1, 0))]
        else:
            text += [(at(line, 1), at(line + 1, 0)), (at(line, 3), at(line, 2))]
            near += [(at(line + 1, 1), at(line, 2))]
            far += [(at(line + 1, 1), at(line + 1, 0)), (at(line + 1, 2), at(line, 3))]
    return (text, near, far)


def back(pairs):
    return [(target, source) for source, target in pairs]


def unit_rows(emb):
    values = emb.astype(jnp.float32)
    norm = jnp.sqrt(jnp.sum(values * values, axis=-1, keepdims=True) + 1e-06)
    return (values / norm, norm)


def unit_bf(emb):
    return unit_rows(emb)[0].astype(jnp.bfloat16)


def back_norm(grad, unit, norm):
    return (grad - unit * jnp.sum(unit * grad, axis=-1, keepdims=True)) / norm


def rows_by_rows(a, b):
    return lax.dot_general(a, b, (((1,), (1,)), ((), ())), preferred_element_type=jnp.float32)


def columns_by_rows(a, b):
    return lax.dot_general(a, b, (((0,), (0,)), ((), ())), preferred_element_type=jnp.float32)


def off_terms(images, texts, s_val, b_val, keep):
    logits = s_val * rows_by_rows(images, texts) + b_val
    loss = jnp.sum(jax.nn.softplus(logits), axis=-1)
    coef = jax.nn.sigmoid(logits).astype(jnp.bfloat16)
    return (jnp.where(keep, coef, 0), jnp.where(keep, loss, 0.0))


def own_terms(images, texts, s_val, b_val):
    logits = s_val * rows_by_rows(images, texts) + b_val
    rows = images.shape[0]
    upper = lax.broadcasted_iota(jnp.int32, (rows, rows), 0)
    lower = lax.broadcasted_iota(jnp.int32, (rows, rows), 1)
    sign = jnp.where(upper == lower, 1.0, -1.0).astype(jnp.float32)
    loss = jnp.sum(jax.nn.softplus(-sign * logits), axis=-1)
    coef = (-sign * jax.nn.sigmoid(-sign * logits)).astype(jnp.bfloat16)
    return (coef, loss)


def shards(image_emb, text_emb, scale, bias):
    text_way, near_way, far_way = routes(lax.axis_size("dp"))
    place = lax.axis_index("group")
    line = lax.axis_index("dp") % RUN
    top = line == RUN - 1
    bottom = line == 0
    leaf = (place == 0) | (place == 3)
    top_two = top & (place == 2)
    hub = ~leaf & ~top_two
    first = bottom & (place == 0)
    seam = first | (top & (place == 3))
    s_val = scale[0]
    b_val = bias[0]
    rows = image_emb.shape[0]

    text_raw = lax.ppermute(text_emb, AXES, text_way)
    image_unit, image_norm = unit_rows(image_emb)
    early, image_norm = lax.optimization_barrier((image_emb, image_norm))
    near_raw = lax.ppermute(early, AXES, near_way)
    text_unit, text_norm = unit_rows(text_emb)
    late, text_norm = lax.optimization_barrier((early, text_norm))
    far_raw = lax.ppermute(late, AXES, far_way)
    image_unit = image_emb.astype(jnp.float32) / image_norm
    text_unit = text_emb.astype(jnp.float32) / text_norm
    images = image_unit.astype(jnp.bfloat16)
    texts = text_unit.astype(jnp.bfloat16)
    coef, loss = own_terms(images, texts, s_val, b_val)
    grad_x = jnp.dot(coef, texts, preferred_element_type=jnp.float32)
    grad_y = columns_by_rows(coef, images)

    other = unit_bf(text_raw)
    c_ri, l_ri = off_terms(images, other, s_val, b_val, leaf)
    grad_x = grad_x + jnp.dot(c_ri, other, preferred_element_type=jnp.float32)

    near = unit_bf(near_raw)
    c_on, l_on = off_terms(near, texts, s_val, b_val, hub | first)
    c_rn, l_rn = off_terms(near, other, s_val, b_val, hub | seam)
    grad_near = s_val * (
        jnp.dot(c_on, texts, preferred_element_type=jnp.float32)
        + jnp.dot(c_rn, other, preferred_element_type=jnp.float32)
    )
    near_back = lax.ppermute(grad_near.astype(jnp.bfloat16), AXES, back(near_way))
    loss_near_back = lax.ppermute(l_on + l_rn, AXES, back(near_way))

    far = unit_bf(far_raw)
    c_of, l_of = off_terms(far, texts, s_val, b_val, hub | (leaf & ~seam))
    c_rf, l_rf = off_terms(far, other, s_val, b_val, hub | seam | top_two)
    grad_far = s_val * (
        jnp.dot(c_of, texts, preferred_element_type=jnp.float32)
        + jnp.dot(c_rf, other, preferred_element_type=jnp.float32)
    )
    far_back = lax.ppermute(grad_far.astype(jnp.bfloat16), AXES, back(far_way))
    grad_other = s_val * (
        columns_by_rows(c_ri, images) + columns_by_rows(c_rn, near) + columns_by_rows(c_rf, far)
    )
    text_back = lax.ppermute(grad_other.astype(jnp.bfloat16), AXES, back(text_way))
    loss_far_back = lax.ppermute(l_of + l_rf, AXES, back(far_way))

    grad_y = s_val * (grad_y + columns_by_rows(c_on, near) + columns_by_rows(c_of, far))
    grad_y = grad_y + text_back.astype(jnp.float32)
    grad_x = s_val * grad_x + near_back.astype(jnp.float32) + far_back.astype(jnp.float32)
    loss = loss + l_ri + loss_near_back + loss_far_back
    row_loss = loss / (HOPS * rows)
    grad_image = back_norm(grad_x, image_unit, image_norm)
    grad_text = back_norm(grad_y, text_unit, text_norm)
    return (row_loss, grad_image, grad_text)


def solution(mesh):
    in_specs = (P(("dp", "group"), None), P(("dp", "group"), None), P(), P())
    out_specs = (P(("dp", "group")), P(("dp", "group"), None), P(("dp", "group"), None))
    return jax.shard_map(shards, mesh=mesh, in_specs=in_specs, out_specs=out_specs, check_vma=False)
```

```python
import jax
import jax.numpy as jnp
from jax import lax
from jax.sharding import PartitionSpec as P

HOPS = 4
GROUP = 4
RUN = 16
AXES = ("dp", "group")


def routes(lines):
    def at(line, place):
        return (line % lines) * GROUP + place

    text, near, far = [], [], []
    for line in range(lines):
        text += [(at(line, 0), at(line, 1)), (at(line, 2), at(line, 3))]
        near += [(at(line, 2), at(line, 1))]
        far += [(at(line, 3), at(line, 1))]
        far += [(at(line + 1, 0), at(line, 2))]
        if line % RUN == RUN - 1:
            text += [(at(line, 3), at(line + 1, 0)), (at(line, 1), at(line, 2))]
            near += [(at(line + 1, 0), at(line, 3)), (at(line + 1, 1), at(line + 1, 0))]
            far += [(at(line + 1, 1), at(line, 3)), (at(line + 1, 2), at(line + 1, 0))]
        else:
            text += [(at(line, 1), at(line + 1, 0)), (at(line, 3), at(line, 2))]
            near += [(at(line + 1, 1), at(line, 2))]
            far += [(at(line + 1, 1), at(line + 1, 0)), (at(line + 1, 2), at(line, 3))]
    return (text, near, far)


def back(pairs):
    return [(target, source) for source, target in pairs]


def unit_rows(emb):
    values = emb.astype(jnp.float32)
    norm = jnp.sqrt(jnp.sum(values * values, axis=-1, keepdims=True) + 1e-06)
    return (values / norm, norm)


def unit_bf(emb):
    return unit_rows(emb)[0].astype(jnp.bfloat16)


def back_norm(grad, unit, norm):
    return (grad - unit * jnp.sum(unit * grad, axis=-1, keepdims=True)) / norm


def rows_by_rows(a, b):
    return lax.dot_general(a, b, (((1,), (1,)), ((), ())), preferred_element_type=jnp.float32)


def columns_by_rows(a, b):
    return lax.dot_general(a, b, (((0,), (0,)), ((), ())), preferred_element_type=jnp.float32)


def off_terms(images, texts, s_val, b_val, keep):
    logits = s_val * rows_by_rows(images, texts) + b_val
    loss = jnp.sum(jax.nn.softplus(logits), axis=-1)
    coef = jax.nn.sigmoid(logits).astype(jnp.bfloat16)
    return (jnp.where(keep, coef, 0), jnp.where(keep, loss, 0.0))


def own_terms(images, texts, s_val, b_val):
    logits = s_val * rows_by_rows(images, texts) + b_val
    rows = images.shape[0]
    upper = lax.broadcasted_iota(jnp.int32, (rows, rows), 0)
    lower = lax.broadcasted_iota(jnp.int32, (rows, rows), 1)
    sign = jnp.where(upper == lower, 1.0, -1.0).astype(jnp.float32)
    loss = jnp.sum(jax.nn.softplus(-sign * logits), axis=-1)
    coef = (-sign * jax.nn.sigmoid(-sign * logits)).astype(jnp.bfloat16)
    return (coef, loss)


def shards(image_emb, text_emb, scale, bias):
    text_way, near_way, far_way = routes(lax.axis_size("dp"))
    place = lax.axis_index("group")
    line = lax.axis_index("dp") % RUN
    top = line == RUN - 1
    bottom = line == 0
    leaf = (place == 0) | (place == 3)
    top_two = top & (place == 2)
    hub = ~leaf & ~top_two
    first = bottom & (place == 0)
    seam = first | (top & (place == 3))
    s_val = scale[0]
    b_val = bias[0]
    rows = image_emb.shape[0]

    text_raw = lax.ppermute(text_emb, AXES, text_way)
    image_unit, image_norm = unit_rows(image_emb)
    early, image_norm = lax.optimization_barrier((image_emb, image_norm))
    near_raw = lax.ppermute(early, AXES, near_way)
    text_unit, text_norm = unit_rows(text_emb)
    late, text_norm = lax.optimization_barrier((early, text_norm))
    far_raw = lax.ppermute(late, AXES, far_way)
    image_unit = image_emb.astype(jnp.float32) / image_norm
    text_unit = text_emb.astype(jnp.float32) / text_norm
    images = image_unit.astype(jnp.bfloat16)
    texts = text_unit.astype(jnp.bfloat16)
    coef, loss = own_terms(images, texts, s_val, b_val)
    grad_x = jnp.dot(coef, texts, preferred_element_type=jnp.float32)
    grad_y = columns_by_rows(coef, images)

    other = unit_bf(text_raw)
    c_ri, l_ri = off_terms(images, other, s_val, b_val, leaf)
    grad_x = grad_x + jnp.dot(c_ri, other, preferred_element_type=jnp.float32)

    near = unit_bf(near_raw)
    c_on, l_on = off_terms(near, texts, s_val, b_val, hub | first)
    c_rn, l_rn = off_terms(near, other, s_val, b_val, hub | seam)
    grad_near = s_val * (
        jnp.dot(c_on, texts, preferred_element_type=jnp.float32)
        + jnp.dot(c_rn, other, preferred_element_type=jnp.float32)
    )
    near_back = lax.ppermute(grad_near.astype(jnp.bfloat16), AXES, back(near_way))

    far = unit_bf(far_raw)
    c_of, l_of = off_terms(far, texts, s_val, b_val, hub | (leaf & ~seam))
    c_rf, l_rf = off_terms(far, other, s_val, b_val, hub | seam | top_two)
    grad_far = s_val * (
        jnp.dot(c_of, texts, preferred_element_type=jnp.float32)
        + jnp.dot(c_rf, other, preferred_element_type=jnp.float32)
    )
    far_back = lax.ppermute(grad_far.astype(jnp.bfloat16), AXES, back(far_way))
    grad_other = s_val * (
        columns_by_rows(c_ri, images) + columns_by_rows(c_rn, near) + columns_by_rows(c_rf, far)
    )
    text_back = lax.ppermute(grad_other.astype(jnp.bfloat16), AXES, back(text_way))

    grad_y = s_val * (grad_y + columns_by_rows(c_on, near) + columns_by_rows(c_of, far))
    grad_y, loss_near, loss_far = lax.optimization_barrier((grad_y, l_on + l_rn, l_of + l_rf))
    loss_near_back = lax.ppermute(loss_near, AXES, back(near_way))
    loss_far_back = lax.ppermute(loss_far, AXES, back(far_way))
    grad_y = grad_y + text_back.astype(jnp.float32)
    grad_x = s_val * grad_x + near_back.astype(jnp.float32) + far_back.astype(jnp.float32)
    loss = loss + l_ri + loss_near_back + loss_far_back
    row_loss = loss / (HOPS * rows)
    grad_image = back_norm(grad_x, image_unit, image_norm)
    grad_text = back_norm(grad_y, text_unit, text_norm)
    return (row_loss, grad_image, grad_text)


def solution(mesh):
    in_specs = (P(("dp", "group"), None), P(("dp", "group"), None), P(), P())
    out_specs = (P(("dp", "group")), P(("dp", "group"), None), P(("dp", "group"), None))
    return jax.shard_map(shards, mesh=mesh, in_specs=in_specs, out_specs=out_specs, check_vma=False)
```

```python
import jax
import jax.numpy as jnp
from jax import lax
from jax.sharding import PartitionSpec as P

HOPS = 4
GROUP = 4
RUN = 16
AXES = ("dp", "group")


def routes(lines):
    def at(line, place):
        return (line % lines) * GROUP + place

    text, near, far = [], [], []
    for line in range(lines):
        text += [(at(line, 0), at(line, 1)), (at(line, 2), at(line, 3))]
        near += [(at(line, 2), at(line, 1))]
        far += [(at(line, 3), at(line, 1))]
        far += [(at(line + 1, 0), at(line, 2))]
        if line % RUN == RUN - 1:
            text += [(at(line, 3), at(line + 1, 0)), (at(line, 1), at(line, 2))]
            near += [(at(line + 1, 0), at(line, 3)), (at(line + 1, 1), at(line + 1, 0))]
            far += [(at(line + 1, 1), at(line, 3)), (at(line + 1, 2), at(line + 1, 0))]
        else:
            text += [(at(line, 1), at(line + 1, 0)), (at(line, 3), at(line, 2))]
            near += [(at(line + 1, 1), at(line, 2))]
            far += [(at(line + 1, 1), at(line + 1, 0)), (at(line + 1, 2), at(line, 3))]
    return (text, near, far)


def back(pairs):
    return [(target, source) for source, target in pairs]


def unit_rows(emb):
    values = emb.astype(jnp.float32)
    norm = jnp.sqrt(jnp.sum(values * values, axis=-1, keepdims=True) + 1e-06)
    return (values / norm, norm)


def unit_bf(emb):
    return unit_rows(emb)[0].astype(jnp.bfloat16)


def back_norm(grad, unit, norm):
    return (grad - unit * jnp.sum(unit * grad, axis=-1, keepdims=True)) / norm


def rows_by_rows(a, b):
    return lax.dot_general(a, b, (((1,), (1,)), ((), ())), preferred_element_type=jnp.float32)


def columns_by_rows(a, b):
    return lax.dot_general(a, b, (((0,), (0,)), ((), ())), preferred_element_type=jnp.float32)


def off_terms(images, texts, s_val, b_val, keep):
    logits = s_val * rows_by_rows(images, texts) + b_val
    loss = jnp.sum(jax.nn.softplus(logits), axis=-1)
    coef = jax.nn.sigmoid(logits).astype(jnp.bfloat16)
    return (jnp.where(keep, coef, 0), jnp.where(keep, loss, 0.0))


def own_terms(images, texts, s_val, b_val):
    logits = s_val * rows_by_rows(images, texts) + b_val
    rows = images.shape[0]
    upper = lax.broadcasted_iota(jnp.int32, (rows, rows), 0)
    lower = lax.broadcasted_iota(jnp.int32, (rows, rows), 1)
    sign = jnp.where(upper == lower, 1.0, -1.0).astype(jnp.float32)
    loss = jnp.sum(jax.nn.softplus(-sign * logits), axis=-1)
    coef = (-sign * jax.nn.sigmoid(-sign * logits)).astype(jnp.bfloat16)
    return (coef, loss)


def shards(image_emb, text_emb, scale, bias):
    text_way, near_way, far_way = routes(lax.axis_size("dp"))
    place = lax.axis_index("group")
    line = lax.axis_index("dp") % RUN
    top = line == RUN - 1
    bottom = line == 0
    leaf = (place == 0) | (place == 3)
    top_two = top & (place == 2)
    hub = ~leaf & ~top_two
    first = bottom & (place == 0)
    seam = first | (top & (place == 3))
    s_val = scale[0]
    b_val = bias[0]
    rows = image_emb.shape[0]

    text_raw = lax.ppermute(text_emb, AXES, text_way)
    image_unit, image_norm = unit_rows(image_emb)
    early, image_norm = lax.optimization_barrier((image_emb, image_norm))
    near_raw = lax.ppermute(early, AXES, near_way)
    text_unit, text_norm = unit_rows(text_emb)
    late = early
    far_raw = lax.ppermute(late, AXES, far_way)
    image_unit = image_emb.astype(jnp.float32) / image_norm
    text_unit = text_emb.astype(jnp.float32) / text_norm
    images = image_unit.astype(jnp.bfloat16)
    texts = text_unit.astype(jnp.bfloat16)
    coef, loss = own_terms(images, texts, s_val, b_val)
    grad_x = jnp.dot(coef, texts, preferred_element_type=jnp.float32)
    grad_y = columns_by_rows(coef, images)

    other = unit_bf(text_raw)
    c_ri, l_ri = off_terms(images, other, s_val, b_val, leaf)
    grad_x = grad_x + jnp.dot(c_ri, other, preferred_element_type=jnp.float32)

    near = unit_bf(near_raw)
    c_on, l_on = off_terms(near, texts, s_val, b_val, hub | first)
    c_rn, l_rn = off_terms(near, other, s_val, b_val, hub | seam)
    grad_near = s_val * (
        jnp.dot(c_on, texts, preferred_element_type=jnp.float32)
        + jnp.dot(c_rn, other, preferred_element_type=jnp.float32)
    )
    near_back = lax.ppermute(grad_near.astype(jnp.bfloat16), AXES, back(near_way))

    far = unit_bf(far_raw)
    c_of, l_of = off_terms(far, texts, s_val, b_val, hub | (leaf & ~seam))
    c_rf, l_rf = off_terms(far, other, s_val, b_val, hub | seam | top_two)
    grad_far = s_val * (
        jnp.dot(c_of, texts, preferred_element_type=jnp.float32)
        + jnp.dot(c_rf, other, preferred_element_type=jnp.float32)
    )
    far_back = lax.ppermute(grad_far.astype(jnp.bfloat16), AXES, back(far_way))
    grad_other = s_val * (
        columns_by_rows(c_ri, images) + columns_by_rows(c_rn, near) + columns_by_rows(c_rf, far)
    )
    text_back = lax.ppermute(grad_other.astype(jnp.bfloat16), AXES, back(text_way))

    grad_y = s_val * (grad_y + columns_by_rows(c_on, near) + columns_by_rows(c_of, far))
    grad_y, loss_near, loss_far = lax.optimization_barrier((grad_y, l_on + l_rn, l_of + l_rf))
    loss_near_back = lax.ppermute(loss_near, AXES, back(near_way))
    loss_far_back = lax.ppermute(loss_far, AXES, back(far_way))
    grad_y = grad_y + text_back.astype(jnp.float32)
    grad_x = s_val * grad_x + near_back.astype(jnp.float32) + far_back.astype(jnp.float32)
    loss = loss + l_ri + loss_near_back + loss_far_back
    row_loss = loss / (HOPS * rows)
    grad_image = back_norm(grad_x, image_unit, image_norm)
    grad_text = back_norm(grad_y, text_unit, text_norm)
    return (row_loss, grad_image, grad_text)


def solution(mesh):
    in_specs = (P(("dp", "group"), None), P(("dp", "group"), None), P(), P())
    out_specs = (P(("dp", "group")), P(("dp", "group"), None), P(("dp", "group"), None))
    return jax.shard_map(shards, mesh=mesh, in_specs=in_specs, out_specs=out_specs, check_vma=False)
```

```python
import jax
import jax.numpy as jnp
from jax import lax
from jax.sharding import PartitionSpec as P

HOPS = 4
GROUP = 4
RUN = 16
AXES = ("dp", "group")


def routes(lines):
    def at(line, place):
        return (line % lines) * GROUP + place

    text, near, far = [], [], []
    for line in range(lines):
        text += [(at(line, 0), at(line, 1)), (at(line, 2), at(line, 3))]
        near += [(at(line, 2), at(line, 1))]
        far += [(at(line, 3), at(line, 1))]
        far += [(at(line + 1, 0), at(line, 2))]
        if line % RUN == RUN - 1:
            text += [(at(line, 3), at(line + 1, 0)), (at(line, 1), at(line, 2))]
            near += [(at(line + 1, 0), at(line, 3)), (at(line + 1, 1), at(line + 1, 0))]
            far += [(at(line + 1, 1), at(line, 3)), (at(line + 1, 2), at(line + 1, 0))]
        else:
            text += [(at(line, 1), at(line + 1, 0)), (at(line, 3), at(line, 2))]
            near += [(at(line + 1, 1), at(line, 2))]
            far += [(at(line + 1, 1), at(line + 1, 0)), (at(line + 1, 2), at(line, 3))]
    return (text, near, far)


def back(pairs):
    return [(target, source) for source, target in pairs]


def unit_rows(emb):
    values = emb.astype(jnp.float32)
    norm = jnp.sqrt(jnp.sum(values * values, axis=-1, keepdims=True) + 1e-06)
    return (values / norm, norm)


def unit_bf(emb):
    return unit_rows(emb)[0].astype(jnp.bfloat16)


def back_norm(grad, unit, norm):
    return (grad - unit * jnp.sum(unit * grad, axis=-1, keepdims=True)) / norm


def rows_by_rows(a, b):
    return lax.dot_general(a, b, (((1,), (1,)), ((), ())), preferred_element_type=jnp.float32)


def columns_by_rows(a, b):
    return lax.dot_general(a, b, (((0,), (0,)), ((), ())), preferred_element_type=jnp.float32)


def off_terms(images, texts, s_val, b_val, keep):
    logits = s_val * rows_by_rows(images, texts) + b_val
    loss = jnp.sum(jax.nn.softplus(logits), axis=-1)
    coef = jax.nn.sigmoid(logits).astype(jnp.bfloat16)
    return (jnp.where(keep, coef, 0), jnp.where(keep, loss, 0.0))


def own_terms(images, texts, s_val, b_val):
    logits = s_val * rows_by_rows(images, texts) + b_val
    rows = images.shape[0]
    upper = lax.broadcasted_iota(jnp.int32, (rows, rows), 0)
    lower = lax.broadcasted_iota(jnp.int32, (rows, rows), 1)
    sign = jnp.where(upper == lower, 1.0, -1.0).astype(jnp.float32)
    loss = jnp.sum(jax.nn.softplus(-sign * logits), axis=-1)
    coef = (-sign * jax.nn.sigmoid(-sign * logits)).astype(jnp.bfloat16)
    return (coef, loss)


def shards(image_emb, text_emb, scale, bias):
    text_way, near_way, far_way = routes(lax.axis_size("dp"))
    place = lax.axis_index("group")
    line = lax.axis_index("dp") % RUN
    top = line == RUN - 1
    bottom = line == 0
    leaf = (place == 0) | (place == 3)
    top_two = top & (place == 2)
    hub = ~leaf & ~top_two
    first = bottom & (place == 0)
    seam = first | (top & (place == 3))
    s_val = scale[0]
    b_val = bias[0]
    rows = image_emb.shape[0]

    text_raw = lax.ppermute(text_emb, AXES, text_way)
    image_unit, image_norm = unit_rows(image_emb)
    early, image_norm = lax.optimization_barrier((image_emb, image_norm))
    near_raw = lax.ppermute(early, AXES, near_way)
    text_unit, text_norm = unit_rows(text_emb)
    late, text_norm = lax.optimization_barrier((early, text_norm))
    far_raw = lax.ppermute(late, AXES, far_way)
    image_unit = image_emb.astype(jnp.float32) / image_norm
    text_unit = text_emb.astype(jnp.float32) / text_norm
    images = image_unit.astype(jnp.bfloat16)
    texts = text_unit.astype(jnp.bfloat16)
    coef, loss = own_terms(images, texts, s_val, b_val)
    grad_x = jnp.dot(coef, texts, preferred_element_type=jnp.float32)
    grad_y = columns_by_rows(coef, images)

    other = unit_bf(text_raw)
    c_ri, l_ri = off_terms(images, other, s_val, b_val, leaf)
    grad_x = grad_x + jnp.dot(c_ri, other, preferred_element_type=jnp.float32)

    near = unit_bf(near_raw)
    c_on, l_on = off_terms(near, texts, s_val, b_val, hub | first)
    c_rn, l_rn = off_terms(near, other, s_val, b_val, hub | seam)
    grad_near = s_val * (
        jnp.dot(c_on, texts, preferred_element_type=jnp.float32)
        + jnp.dot(c_rn, other, preferred_element_type=jnp.float32)
    )

    far = unit_bf(far_raw)
    c_of, l_of = off_terms(far, texts, s_val, b_val, hub | (leaf & ~seam))
    c_rf, l_rf = off_terms(far, other, s_val, b_val, hub | seam | top_two)
    grad_far = s_val * (
        jnp.dot(c_of, texts, preferred_element_type=jnp.float32)
        + jnp.dot(c_rf, other, preferred_element_type=jnp.float32)
    )
    grad_other = s_val * (
        columns_by_rows(c_ri, images) + columns_by_rows(c_rn, near) + columns_by_rows(c_rf, far)
    )
    near_sent, far_sent, other_sent = lax.optimization_barrier(
        (grad_near.astype(jnp.bfloat16), grad_far.astype(jnp.bfloat16), grad_other.astype(jnp.bfloat16))
    )
    text_back = lax.ppermute(other_sent, AXES, back(text_way))
    far_back = lax.ppermute(far_sent, AXES, back(far_way))
    near_back = lax.ppermute(near_sent, AXES, back(near_way))

    grad_y = s_val * (grad_y + columns_by_rows(c_on, near) + columns_by_rows(c_of, far))
    grad_y, loss_near, loss_far = lax.optimization_barrier((grad_y, l_on + l_rn, l_of + l_rf))
    loss_near_back = lax.ppermute(loss_near, AXES, back(near_way))
    loss_far_back = lax.ppermute(loss_far, AXES, back(far_way))
    grad_y = grad_y + text_back.astype(jnp.float32)
    grad_x = s_val * grad_x + near_back.astype(jnp.float32) + far_back.astype(jnp.float32)
    loss = loss + l_ri + loss_near_back + loss_far_back
    row_loss = loss / (HOPS * rows)
    grad_image = back_norm(grad_x, image_unit, image_norm)
    grad_text = back_norm(grad_y, text_unit, text_norm)
    return (row_loss, grad_image, grad_text)


def solution(mesh):
    in_specs = (P(("dp", "group"), None), P(("dp", "group"), None), P(), P())
    out_specs = (P(("dp", "group")), P(("dp", "group"), None), P(("dp", "group"), None))
    return jax.shard_map(shards, mesh=mesh, in_specs=in_specs, out_specs=out_specs, check_vma=False)
```
